32 devices in a mesh: ctx: 8 (over y, x, core), exp: 4 (over z).
Axes of the slice: x: 2, y: 2, z: 4, core: 2. Of those that a mesh axis runs over, the one named last changes fastest.
Arguments:
- inputs: bfloat16 [1024, 1024], P('exp', 'ctx'), may hold values from -6 to 6
- conv_taps: float32 [1024, 31], P('exp'), may hold values from -1 to 1
- norm_gain: bfloat16 [1024], P('exp'), may hold values from 0.099609375 to 1.8984375
- routes: int32 [1024, 2], P('ctx'), may hold values from 0 to 7, all different within a row; in each aligned block of 128 rows (0 to 127, 128 to 255, ...) at most 32 rows name the same one
- gate_probs: float32 [1024, 2], P('ctx'), may hold values from 0.1 to 0.9
- w_gate: bfloat16 [8, 1024, 4096], P('ctx', None, 'exp'), may hold values from -0.1875 to 0.1875
- w_up: bfloat16 [8, 1024, 4096], P('ctx', None, 'exp'), may hold values from -0.1875 to 0.1875
- w_down: bfloat16 [8, 4096, 1024], P('ctx', 'exp'), may hold values from -0.09375 to 0.09375
- grad_out: bfloat16 [1024, 1024], P('exp', 'ctx'), may hold values from -6 to 6
Outputs:
- layer_out: bfloat16 [1024, 1024], P('exp', 'ctx')
- grad_inputs: bfloat16 [1024, 1024], P('exp', 'ctx')
- grad_taps: float32 [1024, 31], P('exp')
- grad_gain: float32 [1024], P('exp')
- grad_gates: float32 [1024, 2], P('ctx')
- grad_w_gate: bfloat16 [8, 1024, 4096], P('ctx', None, 'exp')
- grad_w_up: bfloat16 [8, 1024, 4096], P('ctx', None, 'exp')
- grad_w_down: bfloat16 [8, 4096, 1024], P('ctx', 'exp')
The draws below stay inside these ranges and needn't reach their ends.
Inputs may be any that keep to these rules, and one draw needn't show every extreme that they name: `routes`: in each aligned block of 128 rows (the rows of one index of ctx) no expert is named by more than 32 rows, a bound that some block reaches; the two experts of a row differ.
All inputs are finite; a program needn't handle non-finite values.
Results may differ from the reference program's by a relative error of at most 0.025.
Values may be sent and summed in bfloat16 or wider, within the bound.
A program may use at most 64 MiB of HBM per device.

```python
import math
import jax
import jax.numpy as jnp
import numpy as np
from jax import lax

D = 1024
FF = 4096
TAPS = 31
TOK = 128
EXPERTS = 8
SEQ = 1024
CAP = 32


def block_scale(rng, dims, pieces, smallest, high):
    level = 1.0
    for axis_at, parts in pieces:
        draws = jax.random.uniform(jax.random.fold_in(jax.random.fold_in(rng, 6), axis_at), (parts,), jnp.float32, smallest / len(pieces), high / len(pieces))
        level = level * jnp.repeat(jnp.exp(draws), dims[axis_at] // parts).reshape((-1,) + (1,) * (len(dims) - 1 - axis_at))
    return level


def deal_out(stream_key, own, number, rows, count, top, most, skew):
    sequence = jax.random.permutation(stream_key, count)
    heavy_load, usual = portions_of(count, rows * top, most, skew, True), portions_of(count, rows * top, most, skew, False)
    places = jnp.arange(count)

    def named(sizes, turn):
        used = int((sizes > 0).sum())
        fixed = max(1, used // 4)
        shifted = fixed + (places - fixed + turn * (used - fixed)) % max(1, count - fixed)
        return jnp.zeros((count,), jnp.int32).at[sequence[jnp.where(places < fixed, places, shifted)]].set(jnp.asarray(sizes, jnp.int32))

    sizes = jnp.where(number % 4 == 0, named(heavy_load, number // 4), named(usual, number - number // 4 - 1))
    mixed = jax.random.permutation(jax.random.fold_in(own, 3), count)
    donor, sink = mixed[0:count // 2 * 2:2], mixed[1:count // 2 * 2:2]
    room = jnp.minimum(sizes[donor] - 1, most - sizes[sink]) // 2
    room = jnp.where((donor == sequence[0]) | (sink == sequence[0]) | (sizes[sink] == 0), 0, jnp.maximum(room, 0))
    shifted = jax.random.randint(jax.random.fold_in(own, 4), (count // 2,), 0, 1 << 20) % (room + 1)
    sizes = sizes.at[donor].add(-shifted).at[sink].add(shifted)
    items = jnp.searchsorted(jnp.cumsum(sizes), jnp.arange(rows * top), side="right").astype(jnp.int32)
    grid = items.reshape(top, rows).T
    grid = grid[jax.random.permutation(jax.random.fold_in(own, 1), rows)]
    turn = jax.random.randint(jax.random.fold_in(own, 2), (rows, 1), 0, top)
    return jnp.take_along_axis(grid, (jnp.arange(top)[None, :] + turn) % top, axis=1)


def portions_of(amount, total, reach, lean, full):
    weights = [(1 << 20) // math.isqrt(rank ** lean) + 1 for rank in range(1, amount + 1)]
    largest = reach if full else min(reach, max(-(-total // amount), total * weights[0] // sum(weights)))
    least = 1 if total - largest >= amount - 1 else 0
    counts, spare = [largest] + [least] * (amount - 1), total - largest - least * (amount - 1)
    while spare > 0:
        free = [i for i in range(1, amount) if counts[i] < largest] or [i for i in range(1, amount) if counts[i] < reach]
        mass, remaining = sum([weights[i] for i in free]), spare
        for i in free:
            more = min(reach - counts[i], max(1, remaining * weights[i] // mass), spare)
            counts[i] = counts[i] + more
            spare = spare - more
    return np.array(counts)


def scatter_about(rng, shape, scale, limit, shards=(), kind=jnp.bfloat16):
    loudness = block_scale(rng, shape, shards, -0.22, 0.18) if shards else 1.0
    array = jax.random.normal(rng, shape, jnp.float32) * scale * loudness
    return jnp.minimum(jnp.maximum(array, -limit), limit).astype(kind)


def setup_inputs(seed: int = 0) -> dict:
    splits = jax.random.split(jax.random.key(seed), 10)
    inputs = scatter_about(splits[0], (D, SEQ), 1.0, 6.0, ((0, 4), (1, 8)))
    conv_taps = scatter_about(splits[1], (D, TAPS), TAPS ** -0.5, 1.0, ((0, 4),), jnp.float32)
    norm_gain = jnp.clip(1.0 + 0.18 * jax.random.normal(splits[2], (D,), jnp.float32), 0.099609375, 1.8984375).astype(jnp.bfloat16)
    routes_keys = jax.random.split(jax.random.fold_in(splits[3], 1), SEQ // TOK)
    routes_turns = jax.random.permutation(jax.random.fold_in(splits[3], 3), SEQ // TOK)
    routes = jax.vmap(lambda own, number: deal_out(jax.random.fold_in(splits[3], 2), own, number, TOK, EXPERTS, 2, CAP, 2))(routes_keys, routes_turns).reshape((SEQ, 2))
    gate_probs = jnp.clip(0.1 + 0.79999997 * jax.random.uniform(splits[4], (SEQ, 2), jnp.float32) ** block_scale(splits[4], (SEQ, 2), ((0, 8),), -0.2, 0.2), 0.1, 0.9)
    w_gate = scatter_about(splits[5], (EXPERTS, D, FF), D ** -0.5, 0.1875, ((0, 8), (2, 4)))
    w_up = scatter_about(splits[6], (EXPERTS, D, FF), D ** -0.5, 0.1875, ((0, 8), (2, 4)))
    w_down = scatter_about(splits[7], (EXPERTS, FF, D), FF ** -0.5, 0.09375, ((0, 8), (1, 4)))
    grad_out = scatter_about(splits[8], (D, SEQ), 1.0, 6.0, ((0, 4), (1, 8)))
    return dict(inputs=inputs, conv_taps=conv_taps, norm_gain=norm_gain, routes=routes, gate_probs=gate_probs, w_gate=w_gate, w_up=w_up, w_down=w_down, grad_out=grad_out)


EPS = 1e-05

def expert_pass(operands):
    rows_x, rows_dy, weight_gate, weight_up, weight_down = operands
    gate_act = jnp.dot(rows_x, weight_gate, preferred_element_type=jnp.float32)
    up_act = jnp.dot(rows_x, weight_up, preferred_element_type=jnp.float32)
    sigma = jax.nn.sigmoid(gate_act)
    hidden = (gate_act * sigma * up_act).astype(jnp.bfloat16)
    result = jnp.dot(hidden, weight_down, preferred_element_type=jnp.float32)
    d_hidden = jnp.dot(rows_dy, weight_down.T, preferred_element_type=jnp.float32)
    grad_down = jnp.dot(hidden.T, rows_dy, preferred_element_type=jnp.float32).astype(jnp.bfloat16)
    d_gate = (d_hidden * up_act * sigma * (1.0 + gate_act * (1.0 - sigma))).astype(jnp.bfloat16)
    d_up = (d_hidden * gate_act * sigma).astype(jnp.bfloat16)
    grad_gate = jnp.dot(rows_x.T, d_gate, preferred_element_type=jnp.float32).astype(jnp.bfloat16)
    grad_up = jnp.dot(rows_x.T, d_up, preferred_element_type=jnp.float32).astype(jnp.bfloat16)
    d_rows = jnp.dot(d_gate, weight_gate.T, preferred_element_type=jnp.float32) + jnp.dot(d_up, weight_up.T, preferred_element_type=jnp.float32)
    return (result, grad_gate, grad_up, grad_down, d_rows)

def reference(inputs, conv_taps, norm_gain, routes, gate_probs, w_gate, w_up, w_down, grad_out):
    half = TAPS // 2
    x_full = inputs.astype(jnp.float32)
    padded = jnp.concatenate([x_full[:, SEQ - half:], x_full, x_full[:, :half]], axis=1)
    conv = jnp.zeros((D, SEQ), jnp.float32)
    for offset in range(TAPS):
        conv = conv + conv_taps[:, offset:offset + 1] * padded[:, offset:offset + SEQ]
    mixed = (x_full + conv).astype(jnp.bfloat16)
    mixed_f = mixed.astype(jnp.float32)
    scale = lax.rsqrt(lax.optimization_barrier(jnp.mean(mixed_f * mixed_f, axis=0)) + EPS)
    gain_f = norm_gain.astype(jnp.float32)
    normed = (mixed_f * gain_f[:, None] * scale[None, :]).astype(jnp.bfloat16)
    blocks = SEQ // TOK
    flat = routes.reshape(blocks, 2 * TOK).astype(jnp.int32)
    onehot = (flat[:, :, None] == jnp.arange(EXPERTS, dtype=jnp.int32)[None, None, :]).astype(jnp.int32)
    before = jnp.cumsum(onehot, axis=1, dtype=jnp.int32) - onehot
    place = lax.optimization_barrier(jnp.sum(before * onehot, axis=2, dtype=jnp.int32))
    block_ids = jnp.arange(blocks, dtype=jnp.int32)[:, None]
    dest = (flat * (blocks * CAP) + block_ids * CAP + place).reshape(-1).astype(jnp.int32)
    total = EXPERTS * blocks * CAP
    gates = gate_probs.reshape(-1)
    token_rows = jnp.repeat(normed.T, 2, axis=0)
    cot_f = grad_out.astype(jnp.float32)
    cot_rows = jnp.repeat(cot_f.T, 2, axis=0)
    scaled_rows = (cot_rows * gates[:, None]).astype(jnp.bfloat16)
    dispatched = jnp.zeros((total, D), jnp.bfloat16).at[dest].set(token_rows).reshape(EXPERTS, blocks * CAP, D)
    dy_rows = jnp.zeros((total, D), jnp.bfloat16).at[dest].set(scaled_rows).reshape(EXPERTS, blocks * CAP, D)
    result, grad_gate, grad_up, grad_down, d_rows = lax.map(expert_pass, (dispatched, dy_rows, w_gate, w_up, w_down))
    picked = result.reshape(total, D)[dest]
    moe = lax.optimization_barrier(jnp.sum((picked * gates[:, None]).reshape(SEQ, 2, D), axis=1))
    layer_out = (mixed_f + moe.T).astype(jnp.bfloat16)
    grad_gates = lax.optimization_barrier(jnp.sum(picked * cot_rows, axis=1)).reshape(SEQ, 2)
    d_normed = lax.optimization_barrier(jnp.sum(d_rows.reshape(total, D)[dest].reshape(SEQ, 2, D), axis=1)).T
    grad_gain = lax.optimization_barrier(jnp.sum(d_normed * mixed_f * scale[None, :], axis=1))
    dots = lax.optimization_barrier(jnp.sum(d_normed * gain_f[:, None] * mixed_f, axis=0))
    d_mixed = cot_f + gain_f[:, None] * d_normed * scale[None, :] - mixed_f * (dots * scale * scale * scale / D)[None, :]
    grad_padded = jnp.concatenate([d_mixed[:, SEQ - half:], d_mixed, d_mixed[:, :half]], axis=1)
    grad_in = d_mixed
    tap_parts = []
    for offset in range(TAPS):
        grad_in = grad_in + conv_taps[:, offset:offset + 1] * grad_padded[:, 2 * half - offset:2 * half - offset + SEQ]
        tap_parts.append(lax.optimization_barrier(jnp.sum(d_mixed * padded[:, offset:offset + SEQ], axis=1)))
    grad_taps = jnp.stack(tap_parts, axis=1)
    return (layer_out, grad_in.astype(jnp.bfloat16), grad_taps, grad_gain, grad_gates, grad_gate, grad_up, grad_down)
```

```python
import functools
import jax
import jax.numpy as jnp
from jax import lax
from jax.experimental import pallas as pl
from jax.experimental.pallas import tpu as pltpu
from jax.sharding import PartitionSpec as P

EPS = 1e-05
MESH = pl.DeviceIdType.MESH
F32, BF16 = jnp.float32, jnp.bfloat16
LAST = (((1,), (1,)), ((), ()))
FIRST = (((0,), (0,)), ((), ()))


def greet(n, m):
    c, e = lax.axis_index("ctx"), lax.axis_index("exp")
    barrier = pltpu.get_barrier_semaphore()

    def ctx_peer(k, _):
        pl.semaphore_signal(barrier, inc=1, device_id=(lax.rem(c + k, n), e), device_id_type=MESH)
        return 0

    def exp_peer(k, _):
        pl.semaphore_signal(barrier, inc=1, device_id=(c, lax.rem(e + k, m)), device_id_type=MESH)
        return 0

    lax.fori_loop(1, n, ctx_peer, 0)
    lax.fori_loop(1, m, exp_peer, 0)
    pl.semaphore_wait(barrier, n + m - 2)


class Exchange:
    def __init__(self, axis, size, src, dst, send, recv):
        self.axis, self.size, self.src, self.dst = axis, size, src, dst
        self.send, self.recv = send, recv
        self.me = lax.axis_index(axis)

    def to(self, k):
        peer = lax.rem(self.me + k, self.size)
        if self.axis == "ctx":
            where = (peer, lax.axis_index("exp"))
        else:
            where = (lax.axis_index("ctx"), peer)
        return pltpu.make_async_remote_copy(
            src_ref=self.src(peer),
            dst_ref=self.dst(self.me),
            send_sem=self.send.at[peer],
            recv_sem=self.recv.at[self.me],
            device_id=where,
            device_id_type=MESH,
        )

    def frm(self, k):
        peer = lax.rem(self.me + k, self.size)
        if self.axis == "ctx":
            where = (peer, lax.axis_index("exp"))
        else:
            where = (lax.axis_index("ctx"), peer)
        return pltpu.make_async_remote_copy(
            src_ref=self.src(peer),
            dst_ref=self.dst(peer),
            send_sem=self.send.at[peer],
            recv_sem=self.recv.at[peer],
            device_id=where,
            device_id_type=MESH,
        )

    def each(self, act):
        def body(k, _):
            act(k)
            return 0

        lax.fori_loop(1, self.size, body, 0)

    def start(self):
        self.each(lambda k: self.to(k).start())

    def arrive(self):
        self.each(lambda k: self.frm(k).wait_recv())

    def sent(self):
        self.each(lambda k: self.to(k).wait_send())


class Halo:
    def __init__(self, n, block, left, right, sems):
        c, e = lax.axis_index("ctx"), lax.axis_index("exp")
        up, down = lax.rem(c + 1, n), lax.rem(c + n - 1, n)
        make = pltpu.make_async_remote_copy
        self.copies = [
            make(block, left, sems.at[0], sems.at[1], device_id=(up, e), device_id_type=MESH),
            make(block, right, sems.at[2], sems.at[3], device_id=(down, e), device_id_type=MESH),
        ]

    def start(self):
        for copy in self.copies:
            copy.start()

    def arrive(self):
        for copy in self.copies:
            copy.wait_recv()

    def sent(self):
        for copy in self.copies:
            copy.wait_send()


def shifted(block, left, right, offset, lane):
    width = block.shape[1]
    if offset == 0:
        return block
    if offset > 0:
        return pltpu.roll(jnp.where(lane >= offset, block, right), width - offset, axis=1)
    return pltpu.roll(jnp.where(lane < width + offset, block, left), -offset, axis=1)


def picks(aux, capacity, slots):
    tokens = aux.shape[0]
    lanes = lax.broadcasted_iota(jnp.int32, (tokens, 128), 1)
    named = [aux[:, k : k + 1].astype(jnp.int32) for k in range(2)]
    hot = [(lanes == r).astype(F32) for r in named]
    row = lax.broadcasted_iota(jnp.int32, (tokens, tokens), 0)
    col = lax.broadcasted_iota(jnp.int32, (tokens, tokens), 1)
    earlier = (col < row).astype(F32).astype(BF16)
    count = jnp.dot(earlier, (hot[0] + hot[1]).astype(BF16), preferred_element_type=F32)
    place = lax.broadcasted_iota(jnp.int32, (tokens, slots), 1)
    out = []
    for r, h in zip(named, hot):
        slot = jnp.sum(count * h, axis=1, keepdims=True).astype(jnp.int32)
        out.append((place == r * capacity + slot).astype(F32))
    return out


def front(n, m, taps, capacity, x_ref, pack_ref, aux_ref, cot_ref,
          rx_ref, rdy_ref, mixed_ref, scale_ref, left_ref, right_ref, cots_ref,
          nrm, sq, sx, sdy, hs, cs, cr, qs, qr, ns, nr, ys, yr, xs, xr):
    me, mine = lax.axis_index("ctx"), lax.axis_index("exp")
    chans, tokens = x_ref.shape
    slots, width = sx.shape
    half = taps // 2
    greet(n, m)
    halo = Halo(n, x_ref, left_ref, right_ref, hs)
    halo.start()
    gather_cot = Exchange("exp", m, lambda p: cot_ref, lambda s: cots_ref.at[s], cs, cr)
    gather_cot.start()
    cots_ref[mine] = cot_ref[...]
    aux = aux_ref[...]
    p0, p1 = picks(aux, capacity, slots)
    pt = jnp.transpose(p0 + p1).astype(BF16)
    gated = jnp.transpose(p0 * aux[:, 2:3] + p1 * aux[:, 3:4])
    gate = jnp.sum(gated, axis=1, keepdims=True)

    halo.arrive()
    x = x_ref[...].astype(F32)
    left, right = left_ref[...].astype(F32), right_ref[...].astype(F32)
    pack = pack_ref[...]
    lane = lax.broadcasted_iota(jnp.int32, (chans, tokens), 1)
    conv = jnp.zeros((chans, tokens), F32)
    for j in range(taps):
        conv = conv + pack[:, j : j + 1] * shifted(x, left, right, j - half, lane)
    mixed = (x + conv).astype(BF16)
    mixed_ref[...] = mixed
    mixed = mixed.astype(F32)
    sq[mine] = jnp.broadcast_to(jnp.sum(mixed * mixed, axis=0, keepdims=True), (8, tokens))
    squares = Exchange("exp", m, lambda p: sq.at[mine], lambda s: sq.at[s], qs, qr)
    squares.start()

    def rows(ref):
        return lambda p: ref.at[pl.ds(pl.multiple_of(p * capacity, capacity), capacity)]

    own = pl.ds(pl.multiple_of(me * capacity, capacity), capacity)
    gather_cot.arrive()
    for k in range(m):
        part = lax.dot_general(pt, cots_ref[k], LAST, preferred_element_type=F32)
        sdy[:, k * chans : (k + 1) * chans] = (part * gate).astype(BF16)
    send_dy = Exchange("ctx", n, rows(sdy), rows(rdy_ref), ys, yr)
    squares.arrive()
    total = jnp.sum(sq[...], axis=0)
    scale = lax.rsqrt(total / width + EPS)
    scale_ref[...] = scale
    nrm[mine] = (mixed * pack[:, taps : taps + 1] * scale[:1]).astype(BF16)
    gather_x = Exchange("exp", m, lambda p: nrm.at[mine], lambda s: nrm.at[s], ns, nr)
    gather_x.start()
    send_dy.start()
    rdy_ref[own, :] = sdy[own, :]
    gather_x.arrive()
    for k in range(m):
        part = lax.dot_general(pt, nrm[k], LAST, preferred_element_type=F32)
        sx[:, k * chans : (k + 1) * chans] = part.astype(BF16)
    send_x = Exchange("ctx", n, rows(sx), rows(rx_ref), xs, xr)
    send_x.start()
    rx_ref[own, :] = sx[own, :]
    send_dy.arrive()
    send_x.arrive()
    for done in (halo, gather_cot, squares, send_dy, gather_x, send_x):
        done.sent()


def back(n, m, taps, capacity, y_ref, dx_ref, x_ref, left_ref, right_ref, pack_ref, aux_ref, cot_ref,
         cots_ref, mixed_ref, scale_ref,
         out_ref, gin_ref, tap_ref, gg_ref,
         by, bdx, zdx, zy, rdx, ry, dots, norm, dm, dl, dr, tp,
         ds_, dr_, ys, yr, as_, ar, bs, br, gs, gr, qs, qr, hs, ts, tr):
    me, mine = lax.axis_index("ctx"), lax.axis_index("exp")
    chans, tokens = x_ref.shape
    slots, width = by.shape
    half = taps // 2
    greet(n, m)

    def rows(ref):
        return lambda p: ref.at[pl.ds(pl.multiple_of(p * capacity, capacity), capacity)]

    own = pl.ds(pl.multiple_of(me * capacity, capacity), capacity)
    send_dx = Exchange("ctx", n, rows(dx_ref), rows(bdx), ds_, dr_)
    send_y = Exchange("ctx", n, rows(y_ref), rows(by), ys, yr)
    send_dx.start()
    send_y.start()
    bdx[own, :] = dx_ref[own, :]
    by[own, :] = y_ref[own, :]
    aux = aux_ref[...]
    p0, p1 = picks(aux, capacity, slots)
    both = (p0 + p1).astype(BF16)
    p0, p1 = p0.astype(BF16), p1.astype(BF16)
    x = x_ref[...].astype(F32)
    left, right = left_ref[...].astype(F32), right_ref[...].astype(F32)
    mixed = mixed_ref[...].astype(F32)
    pack = pack_ref[...]
    gain = pack[:, taps : taps + 1]
    scale = scale_ref[:1]
    cot = cot_ref[...].astype(F32)

    send_dx.arrive()
    for k in range(m):
        part = jnp.dot(both, bdx[:, k * chans : (k + 1) * chans], preferred_element_type=F32)
        zdx[k] = part.astype(BF16)
    sum_dx = Exchange("exp", m, lambda p: zdx.at[p], lambda s: rdx.at[s], as_, ar)
    sum_dx.start()
    rdx[mine] = zdx[mine]
    send_y.arrive()
    d0 = jnp.zeros((tokens, 1), F32)
    d1 = jnp.zeros((tokens, 1), F32)
    for k in range(m):
        block = by[:, k * chans : (k + 1) * chans]
        y0 = jnp.dot(p0, block, preferred_element_type=F32)
        y1 = jnp.dot(p1, block, preferred_element_type=F32)
        zy[k] = (y0 * aux[:, 2:3] + y1 * aux[:, 3:4]).astype(BF16)
        turned = jnp.transpose(cots_ref[k].astype(F32))
        d0 = d0 + jnp.sum(y0 * turned, axis=1, keepdims=True)
        d1 = d1 + jnp.sum(y1 * turned, axis=1, keepdims=True)
    sum_y = Exchange("exp", m, lambda p: zy.at[p], lambda s: ry.at[s], bs, br)
    sum_y.start()
    ry[mine] = zy[mine]
    col = lax.broadcasted_iota(jnp.int32, (tokens, 128), 1)
    dots[mine] = jnp.transpose(jnp.where(col == 0, d0, jnp.where(col == 1, d1, 0.0)))[:8]
    sum_dots = Exchange("exp", m, lambda p: dots.at[mine], lambda s: dots.at[s], gs, gr)
    sum_dots.start()

    sum_dx.arrive()
    dn = jnp.transpose(jnp.sum(rdx[...].astype(F32), axis=0))
    weighted = dn * mixed
    norm[mine] = jnp.broadcast_to(jnp.sum(weighted * gain, axis=0, keepdims=True), (8, tokens))
    sum_norm = Exchange("exp", m, lambda p: norm.at[mine], lambda s: norm.at[s], qs, qr)
    sum_norm.start()
    lane = lax.broadcasted_iota(jnp.int32, (chans, tokens), 1)
    gain_grad = jnp.sum(weighted * scale, axis=1, keepdims=True)
    sum_norm.arrive()
    q = jnp.sum(norm[...], axis=0)[:1]
    d_mixed = cot + gain * dn * scale - mixed * (q * scale * scale * scale / width)
    dm[...] = d_mixed.astype(BF16)
    halo = Halo(n, dm, dl, dr, hs)
    halo.start()
    grads = jnp.where(lane == taps, gain_grad, 0.0)
    for j in range(taps):
        term = jnp.sum(d_mixed * shifted(x, left, right, j - half, lane), axis=1, keepdims=True)
        grads = jnp.where(lane == j, term, grads)
    tp[me] = jnp.transpose(grads)[: tp.shape[1]]
    sum_taps = Exchange("ctx", n, lambda p: tp.at[me], lambda s: tp.at[s], ts, tr)
    sum_taps.start()
    halo.arrive()
    dleft, dright = dl[...].astype(F32), dr[...].astype(F32)
    grad = d_mixed
    for j in range(taps):
        grad = grad + pack[:, j : j + 1] * shifted(d_mixed, dleft, dright, half - j, lane)
    gin_ref[...] = grad.astype(BF16)
    sum_y.arrive()
    out_ref[...] = (mixed + jnp.transpose(jnp.sum(ry[...].astype(F32), axis=0))).astype(BF16)
    sum_dots.arrive()
    gg_ref[...] = jnp.sum(dots[...], axis=0)
    sum_taps.arrive()
    tap_ref[...] = jnp.sum(tp[...], axis=0)
    for done in (send_dx, send_y, sum_dx, sum_y, sum_dots, sum_norm, halo, sum_taps):
        done.sent()


def sems(*counts):
    out = []
    for count in counts:
        out += [pltpu.SemaphoreType.DMA((count,)), pltpu.SemaphoreType.DMA((count,))]
    return out


def local(inputs, conv_taps, norm_gain, routes, gate_probs, w_gate, w_up, w_down, grad_out):
    chans, tokens = inputs.shape
    taps = conv_taps.shape[1]
    width = w_gate.shape[1]
    n, m = lax.axis_size("ctx"), lax.axis_size("exp")
    capacity = max(tokens // 8, (2 * tokens + n - 1) // n)
    slots = n * capacity
    pad = -(-(taps + 1) // 8) * 8
    pack = jnp.concatenate([conv_taps, norm_gain.astype(F32)[:, None]], axis=1)
    aux = jnp.concatenate([routes.astype(F32), gate_probs], axis=1)
    vmem = pl.BlockSpec(memory_space=pltpu.VMEM)
    shape = jax.ShapeDtypeStruct
    rx, rdy, mixed, scale, left, right, cots = pl.pallas_call(
        functools.partial(front, n, m, taps, capacity),
        out_shape=(
            shape((slots, width), BF16),
            shape((slots, width), BF16),
            shape((chans, tokens), BF16),
            shape((8, tokens), F32),
            shape((chans, tokens), BF16),
            shape((chans, tokens), BF16),
            shape((m, chans, tokens), BF16),
        ),
        in_specs=[vmem] * 4,
        out_specs=(vmem,) * 7,
        scratch_shapes=[
            pltpu.VMEM((m, chans, tokens), BF16),
            pltpu.VMEM((m, 8, tokens), F32),
            pltpu.VMEM((slots, width), BF16),
            pltpu.VMEM((slots, width), BF16),
            pltpu.SemaphoreType.DMA((4,)),
            *sems(m, m, m, n, n),
        ],
        compiler_params=pltpu.CompilerParams(
            collective_id=0, has_side_effects=True, vmem_limit_bytes=40 << 20
        ),
        name="front",
    )(inputs, pack, aux, grad_out)
    weight_gate, weight_up, weight_down = w_gate[0], w_up[0], w_down[0]
    gate_act = jnp.dot(rx, weight_gate, preferred_element_type=F32)
    up_act = jnp.dot(rx, weight_up, preferred_element_type=F32)
    sigma = jax.nn.sigmoid(gate_act)
    hidden = (gate_act * sigma * up_act).astype(BF16)
    result = jnp.dot(hidden, weight_down, preferred_element_type=F32).astype(BF16)
    d_hidden = lax.dot_general(rdy, weight_down, LAST, preferred_element_type=F32)
    d_gate = (d_hidden * up_act * sigma * (1.0 + gate_act * (1.0 - sigma))).astype(BF16)
    d_up = (d_hidden * gate_act * sigma).astype(BF16)
    d_rows = lax.dot_general(d_gate, weight_gate, LAST, preferred_element_type=F32)
    d_rows = d_rows + lax.dot_general(d_up, weight_up, LAST, preferred_element_type=F32)
    d_rows = d_rows.astype(BF16)
    grad_down = lax.dot_general(hidden, rdy, FIRST, preferred_element_type=F32).astype(BF16)
    grad_gate = lax.dot_general(rx, d_gate, FIRST, preferred_element_type=F32).astype(BF16)
    grad_up = lax.dot_general(rx, d_up, FIRST, preferred_element_type=F32).astype(BF16)
    layer_out, grad_in, tap_sum, gate_sum = pl.pallas_call(
        functools.partial(back, n, m, taps, capacity),
        out_shape=(
            shape((chans, tokens), BF16),
            shape((chans, tokens), BF16),
            shape((pad, chans), F32),
            shape((8, tokens), F32),
        ),
        in_specs=[vmem] * 11,
        out_specs=(vmem,) * 4,
        scratch_shapes=[
            pltpu.VMEM((slots, width), BF16),
            pltpu.VMEM((slots, width), BF16),
            pltpu.VMEM((m, tokens, chans), BF16),
            pltpu.VMEM((m, tokens, chans), BF16),
            pltpu.VMEM((m, tokens, chans), BF16),
            pltpu.VMEM((m, tokens, chans), BF16),
            pltpu.VMEM((m, 8, tokens), F32),
            pltpu.VMEM((m, 8, tokens), F32),
            pltpu.VMEM((chans, tokens), BF16),
            pltpu.VMEM((chans, tokens), BF16),
            pltpu.VMEM((chans, tokens), BF16),
            pltpu.VMEM((n, pad, chans), F32),
            *sems(n, n, m, m, m, m),
            pltpu.SemaphoreType.DMA((4,)),
            *sems(n),
        ],
        compiler_params=pltpu.CompilerParams(
            collective_id=1, has_side_effects=True, vmem_limit_bytes=40 << 20
        ),
        name="back",
    )(result, d_rows, inputs, left, right, pack, aux, grad_out, cots, mixed, scale)
    return (
        layer_out,
        grad_in,
        tap_sum[:taps].T,
        tap_sum[taps],
        gate_sum[:2].T,
        grad_gate[None],
        grad_up[None],
        grad_down[None],
    )


def solution(mesh):
    return jax.shard_map(
        local,
        mesh=mesh,
        in_specs=(
            P("exp", "ctx"),
            P("exp", None),
            P("exp"),
            P("ctx", None),
            P("ctx", None),
            P("ctx", None, "exp"),
            P("ctx", None, "exp"),
            P("ctx", "exp", None),
            P("exp", "ctx"),
        ),
        out_specs=(
            P("exp", "ctx"),
            P("exp", "ctx"),
            P("exp", None),
            P("exp"),
            P("ctx", None),
            P("ctx", None, "exp"),
            P("ctx", None, "exp"),
            P("ctx", "exp", None),
        ),
        check_vma=False,
    )
```

```python
import functools
import jax
import jax.numpy as jnp
from jax import lax
from jax.experimental import pallas as pl
from jax.experimental.pallas import tpu as pltpu
from jax.sharding import PartitionSpec as P

EPS = 1e-05
MESH = pl.DeviceIdType.MESH
F32, BF16 = jnp.float32, jnp.bfloat16
LAST = (((1,), (1,)), ((), ()))
FIRST = (((0,), (0,)), ((), ()))


def greet(n, m):
    c, e = lax.axis_index("ctx"), lax.axis_index("exp")
    barrier = pltpu.get_barrier_semaphore()

    def ctx_peer(k, _):
        pl.semaphore_signal(barrier, inc=1, device_id=(lax.rem(c + k, n), e), device_id_type=MESH)
        return 0

    def exp_peer(k, _):
        pl.semaphore_signal(barrier, inc=1, device_id=(c, lax.rem(e + k, m)), device_id_type=MESH)
        return 0

    lax.fori_loop(1, n, ctx_peer, 0)
    lax.fori_loop(1, m, exp_peer, 0)
    pl.semaphore_wait(barrier, n + m - 2)


class Exchange:
    def __init__(self, axis, size, src, dst, send, recv):
        self.axis, self.size, self.src, self.dst = axis, size, src, dst
        self.send, self.recv = send, recv
        self.me = lax.axis_index(axis)

    def to(self, k):
        peer = lax.rem(self.me + k, self.size)
        if self.axis == "ctx":
            where = (peer, lax.axis_index("exp"))
        else:
            where = (lax.axis_index("ctx"), peer)
        return pltpu.make_async_remote_copy(
            src_ref=self.src(peer),
            dst_ref=self.dst(self.me),
            send_sem=self.send.at[peer],
            recv_sem=self.recv.at[self.me],
            device_id=where,
            device_id_type=MESH,
        )

    def frm(self, k):
        peer = lax.rem(self.me + k, self.size)
        if self.axis == "ctx":
            where = (peer, lax.axis_index("exp"))
        else:
            where = (lax.axis_index("ctx"), peer)
        return pltpu.make_async_remote_copy(
            src_ref=self.src(peer),
            dst_ref=self.dst(peer),
            send_sem=self.send.at[peer],
            recv_sem=self.recv.at[peer],
            device_id=where,
            device_id_type=MESH,
        )

    def each(self, act):
        def body(k, _):
            act(k)
            return 0

        lax.fori_loop(1, self.size, body, 0)

    def start(self):
        self.each(lambda k: self.to(k).start())

    def arrive(self):
        self.each(lambda k: self.frm(k).wait_recv())

    def sent(self):
        self.each(lambda k: self.to(k).wait_send())


class Halo:
    def __init__(self, n, block, left, right, sems):
        c, e = lax.axis_index("ctx"), lax.axis_index("exp")
        up, down = lax.rem(c + 1, n), lax.rem(c + n - 1, n)
        make = pltpu.make_async_remote_copy
        self.copies = [
            make(block, left, sems.at[0], sems.at[1], device_id=(up, e), device_id_type=MESH),
            make(block, right, sems.at[2], sems.at[3], device_id=(down, e), device_id_type=MESH),
        ]

    def start(self):
        for copy in self.copies:
            copy.start()

    def arrive(self):
        for copy in self.copies:
            copy.wait_recv()

    def sent(self):
        for copy in self.copies:
            copy.wait_send()


def shifted(block, left, right, offset, lane):
    width = block.shape[1]
    if offset == 0:
        return block
    if offset > 0:
        return pltpu.roll(jnp.where(lane >= offset, block, right), width - offset, axis=1)
    return pltpu.roll(jnp.where(lane < width + offset, block, left), -offset, axis=1)


def picks(routes, capacity, slots):
    tokens = routes.shape[1]
    names = lax.broadcasted_iota(jnp.int32, (128, tokens), 0)
    named = [routes[k : k + 1] for k in range(2)]
    hot = [(names == r).astype(F32) for r in named]
    row = lax.broadcasted_iota(jnp.int32, (tokens, tokens), 0)
    col = lax.broadcasted_iota(jnp.int32, (tokens, tokens), 1)
    earlier = (row < col).astype(F32).astype(BF16)
    count = jnp.dot((hot[0] + hot[1]).astype(BF16), earlier, preferred_element_type=F32)
    place = lax.broadcasted_iota(jnp.int32, (slots, tokens), 0)
    out = []
    for r, h in zip(named, hot):
        slot = jnp.sum(count * h, axis=0, keepdims=True).astype(jnp.int32)
        out.append((place == r * capacity + slot).astype(F32))
    return out


def columns(taps_ref, gain_ref, pad):
    taps, chans = taps_ref.shape
    gain = gain_ref[...].astype(F32)
    rows = [taps_ref[...], gain]
    if pad > taps + 1:
        rows.append(jnp.zeros((pad - taps - 1, chans), F32))
    return jnp.transpose(jnp.concatenate(rows, axis=0))


def parts(n, m, capacity, src, dst, send, recv):
    def rows(ref, k):
        return lambda p: ref.at[k, pl.ds(pl.multiple_of(p * capacity, capacity), capacity)]

    return [Exchange("ctx", n, rows(src, k), rows(dst, k), send.at[k], recv.at[k]) for k in range(m)]


def front(n, m, capacity, pad, x_ref, taps_ref, gain_ref, routes_ref, gates_ref, cot_ref,
          rx_ref, rdy_ref, mixed_ref, scale_ref, left_ref, right_ref, cots_ref,
          nrm, sq, sx, sdy, gx, gdy, hs, cs, cr, qs, qr, ns, nr, ys, yr, xs, xr):
    me, mine = lax.axis_index("ctx"), lax.axis_index("exp")
    chans, tokens = x_ref.shape
    slots, width = rx_ref.shape
    taps = taps_ref.shape[0]
    half = taps // 2
    greet(n, m)
    halo = Halo(n, x_ref, left_ref, right_ref, hs)
    halo.start()
    gather_cot = Exchange("exp", m, lambda p: cot_ref, lambda s: cots_ref.at[s], cs, cr)
    gather_cot.start()
    cots_ref[mine] = cot_ref[...]
    p0, p1 = picks(routes_ref[...], capacity, slots)
    pt = (p0 + p1).astype(BF16)
    gates = gates_ref[...]
    gate = jnp.sum(p0 * gates[:1] + p1 * gates[1:], axis=1, keepdims=True)
    pack = columns(taps_ref, gain_ref, pad)
    own = pl.ds(pl.multiple_of(me * capacity, capacity), capacity)

    halo.arrive()
    x = x_ref[...].astype(F32)
    left, right = left_ref[...].astype(F32), right_ref[...].astype(F32)
    lane = lax.broadcasted_iota(jnp.int32, (chans, tokens), 1)
    conv = jnp.zeros((chans, tokens), F32)
    for j in range(taps):
        conv = conv + pack[:, j : j + 1] * shifted(x, left, right, j - half, lane)
    mixed = (x + conv).astype(BF16)
    mixed_ref[...] = mixed
    mixed = mixed.astype(F32)
    sq[mine] = jnp.broadcast_to(jnp.sum(mixed * mixed, axis=0, keepdims=True), (8, tokens))
    squares = Exchange("exp", m, lambda p: sq.at[mine], lambda s: sq.at[s], qs, qr)
    squares.start()

    send_dy = parts(n, m, capacity, sdy, gdy, ys, yr)
    gather_cot.arrive()
    for k in range(m):
        part = lax.dot_general(pt, cots_ref[k], LAST, preferred_element_type=F32)
        sdy[k] = (part * gate).astype(BF16)
        send_dy[k].start()
        gdy[k, own] = sdy[k, own]
    squares.arrive()
    scale = lax.rsqrt(jnp.sum(sq[...], axis=0) / width + EPS)
    scale_ref[...] = scale
    nrm[mine] = (mixed * pack[:, taps : taps + 1] * scale[:1]).astype(BF16)
    gather_x = Exchange("exp", m, lambda p: nrm.at[mine], lambda s: nrm.at[s], ns, nr)
    gather_x.start()

    def part_of(k):
        k = lax.rem(mine + k, m)
        part = lax.dot_general(pt, nrm[k], LAST, preferred_element_type=F32)
        sx[k] = part.astype(BF16)
        rows = lambda ref: lambda p: ref.at[k, pl.ds(pl.multiple_of(p * capacity, capacity), capacity)]
        return Exchange("ctx", n, rows(sx), rows(gx), xs.at[k], xr.at[k]), k

    def forward(k):
        send, k = part_of(k)
        send.start()
        gx[k, own] = sx[k, own]

    forward(0)
    for k in range(1, m):
        gather_x.frm(k).wait_recv()
        forward(k)
    send_x = parts(n, m, capacity, sx, gx, xs, xr)
    for k in range(m):
        send_dy[k].arrive()
        rdy_ref[:, k * chans : (k + 1) * chans] = gdy[k]
    for k in range(m):
        send_x[k].arrive()
        rx_ref[:, k * chans : (k + 1) * chans] = gx[k]
    for done in (halo, gather_cot, squares, gather_x, *send_dy, *send_x):
        done.sent()


def grad_into(out_ref, lhs_ref, rhs_ref, tile):
    right = rhs_ref[...]

    def body(i, _):
        at = pl.ds(pl.multiple_of(i * tile, tile), tile)
        out_ref[at, :] = lax.dot_general(
            lhs_ref[:, at], right, FIRST, preferred_element_type=F32
        ).astype(BF16)
        return 0

    lax.fori_loop(0, lhs_ref.shape[1] // tile, body, 0)


def back(n, m, capacity, pad, y_ref, dx_ref, rx_ref, rdy_ref, hidden_ref, dgate_ref, dup_ref,
         x_ref, left_ref, right_ref, taps_ref, gain_ref, routes_ref, gates_ref,
         cot_ref, cots_ref, mixed_ref, scale_ref,
         out_ref, gin_ref, tap_ref, gain_out_ref, gg_ref, gwg_ref, gwu_ref, gwd_ref,
         by, bdx, sy, sdx, zdx, zy, rdx, ry, dots, norm, dm, dl, dr, tp,
         ds_, dr_, ys, yr, as_, ar, bs, br, gs, gr, qs, qr, hs, ts, tr):
    me, mine = lax.axis_index("ctx"), lax.axis_index("exp")
    chans, tokens = x_ref.shape
    slots, width = y_ref.shape
    taps = taps_ref.shape[0]
    half = taps // 2
    greet(n, m)
    own = pl.ds(pl.multiple_of(me * capacity, capacity), capacity)
    send_dx = parts(n, m, capacity, sdx, bdx, ds_, dr_)
    send_y = parts(n, m, capacity, sy, by, ys, yr)
    for k in range(m):
        sdx[k] = dx_ref[:, k * chans : (k + 1) * chans]
        send_dx[k].start()
        bdx[k, own] = sdx[k, own]
    for k in range(m):
        sy[k] = y_ref[:, k * chans : (k + 1) * chans]
        send_y[k].start()
        by[k, own] = sy[k, own]
    t0, t1 = picks(routes_ref[...], capacity, slots)
    p0, p1 = jnp.transpose(t0), jnp.transpose(t1)
    both = (p0 + p1).astype(BF16)
    gates = jnp.transpose(jnp.concatenate([gates_ref[...], jnp.zeros((6, tokens), F32)], axis=0))
    g0, g1 = gates[:, :1], gates[:, 1:2]
    p0, p1 = p0.astype(BF16), p1.astype(BF16)
    pack = columns(taps_ref, gain_ref, pad)
    grad_into(gwd_ref, hidden_ref, rdy_ref, min(256, hidden_ref.shape[1]))
    sum_dx = Exchange("exp", m, lambda p: zdx.at[p], lambda s: rdx.at[s], as_, ar)
    sum_y = Exchange("exp", m, lambda p: zy.at[p], lambda s: ry.at[s], bs, br)

    def when_other(k, exchange):
        @pl.when(mine != k)
        def _():
            exchange.to(lax.rem(k - mine + m, m)).start()

    for k in range(m):
        send_dx[k].arrive()
        zdx[k] = jnp.dot(both, bdx[k], preferred_element_type=F32).astype(BF16)
        when_other(k, sum_dx)
    rdx[mine] = zdx[mine]
    grad_into(gwg_ref, rx_ref, dgate_ref, min(256, width))
    x = x_ref[...].astype(F32)
    left, right = left_ref[...].astype(F32), right_ref[...].astype(F32)
    mixed = mixed_ref[...].astype(F32)
    gain = pack[:, taps : taps + 1]
    scale = scale_ref[:1]
    cot = cot_ref[...].astype(F32)
    sum_dx.arrive()
    dn = jnp.transpose(jnp.sum(rdx[...].astype(F32), axis=0))
    weighted = dn * mixed
    norm[mine] = jnp.broadcast_to(jnp.sum(weighted * gain, axis=0, keepdims=True), (8, tokens))
    sum_norm = Exchange("exp", m, lambda p: norm.at[mine], lambda s: norm.at[s], qs, qr)
    sum_norm.start()
    d0 = jnp.zeros((tokens, 1), F32)
    d1 = jnp.zeros((tokens, 1), F32)
    for k in range(m):
        send_y[k].arrive()
        y0 = jnp.dot(p0, by[k], preferred_element_type=F32)
        y1 = jnp.dot(p1, by[k], preferred_element_type=F32)
        zy[k] = (y0 * g0 + y1 * g1).astype(BF16)
        when_other(k, sum_y)
        turned = jnp.transpose(cots_ref[k].astype(F32))
        d0 = d0 + jnp.sum(y0 * turned, axis=1, keepdims=True)
        d1 = d1 + jnp.sum(y1 * turned, axis=1, keepdims=True)
    ry[mine] = zy[mine]
    col = lax.broadcasted_iota(jnp.int32, (tokens, 128), 1)
    dots[mine] = jnp.transpose(jnp.where(col == 0, d0, jnp.where(col == 1, d1, 0.0)))[:8]
    sum_dots = Exchange("exp", m, lambda p: dots.at[mine], lambda s: dots.at[s], gs, gr)
    sum_dots.start()
    lane = lax.broadcasted_iota(jnp.int32, (chans, tokens), 1)
    gain_grad = jnp.sum(weighted * scale, axis=1, keepdims=True)
    sum_norm.arrive()
    q = jnp.sum(norm[...], axis=0)[:1]
    d_mixed = cot + gain * dn * scale - mixed * (q * scale * scale * scale / width)
    dm[...] = d_mixed.astype(BF16)
    halo = Halo(n, dm, dl, dr, hs)
    halo.start()
    grads = jnp.where(lane == taps, gain_grad, 0.0)
    for j in range(taps):
        term = jnp.sum(d_mixed * shifted(x, left, right, j - half, lane), axis=1, keepdims=True)
        grads = jnp.where(lane == j, term, grads)
    tp[me] = jnp.transpose(grads)[:pad]
    sum_taps = Exchange("ctx", n, lambda p: tp.at[me], lambda s: tp.at[s], ts, tr)
    sum_taps.start()
    halo.arrive()
    dleft, dright = dl[...].astype(F32), dr[...].astype(F32)
    grad = d_mixed
    for j in range(taps):
        grad = grad + pack[:, j : j + 1] * shifted(d_mixed, dleft, dright, half - j, lane)
    gin_ref[...] = grad.astype(BF16)
    grad_into(gwu_ref, rx_ref, dup_ref, min(256, width))
    sum_y.arrive()
    out_ref[...] = (mixed + jnp.transpose(jnp.sum(ry[...].astype(F32), axis=0))).astype(BF16)
    sum_dots.arrive()
    gg_ref[...] = jnp.sum(dots[...], axis=0)[:2]
    sum_taps.arrive()
    total = jnp.sum(tp[...], axis=0)
    tap_ref[...] = total[:taps]
    gain_out_ref[...] = total[taps : taps + 1]
    for done in (*send_dx, *send_y, sum_dx, sum_y, sum_dots, sum_norm, halo, sum_taps):
        done.sent()


def hand_on(count, *refs):
    done = refs[2 * count]
    copies = [pltpu.make_async_copy(refs[i], refs[count + i], done.at[i]) for i in range(count)]
    for copy in copies:
        copy.start()
    for copy in copies:
        copy.wait()


def sems(*counts):
    out = []
    for count in counts:
        shape = count if isinstance(count, tuple) else (count,)
        out += [pltpu.SemaphoreType.DMA(shape), pltpu.SemaphoreType.DMA(shape)]
    return out


def local(inputs, conv_taps, norm_gain, routes, gate_probs, w_gate, w_up, w_down, grad_out):
    chans, tokens = inputs.shape
    taps = conv_taps.shape[1]
    width = w_gate.shape[1]
    n, m = lax.axis_size("ctx"), lax.axis_size("exp")
    capacity = max(tokens // 8, (2 * tokens + n - 1) // n)
    slots = n * capacity
    pad = -(-(taps + 1) // 8) * 8
    taps_t, gain_row = conv_taps.T, norm_gain.reshape(1, chans)
    routes_t, gates_t = routes.T, gate_probs.T
    vmem = pl.BlockSpec(memory_space=pltpu.VMEM)
    shape = jax.ShapeDtypeStruct
    rx, rdy, mixed, scale, left, right, cots = pl.pallas_call(
        functools.partial(front, n, m, capacity, pad),
        out_shape=(
            shape((slots, width), BF16),
            shape((slots, width), BF16),
            shape((chans, tokens), BF16),
            shape((8, tokens), F32),
            shape((chans, tokens), BF16),
            shape((chans, tokens), BF16),
            shape((m, chans, tokens), BF16),
        ),
        in_specs=[vmem] * 6,
        out_specs=(vmem,) * 7,
        scratch_shapes=[
            pltpu.VMEM((m, chans, tokens), BF16),
            pltpu.VMEM((m, 8, tokens), F32),
            *[pltpu.VMEM((m, slots, chans), BF16)] * 4,
            pltpu.SemaphoreType.DMA((4,)),
            *sems(m, m, m, (m, n), (m, n)),
        ],
        compiler_params=pltpu.CompilerParams(
            collective_id=0, has_side_effects=True, vmem_limit_bytes=40 << 20
        ),
        name="front",
    )(inputs, taps_t, gain_row, routes_t, gates_t, grad_out)
    weight_gate, weight_up, weight_down = w_gate[0], w_up[0], w_down[0]
    gate_act = jnp.dot(rx, weight_gate, preferred_element_type=F32)
    up_act = jnp.dot(rx, weight_up, preferred_element_type=F32)
    sigma = jax.nn.sigmoid(gate_act)
    hidden = (gate_act * sigma * up_act).astype(BF16)
    result = jnp.dot(hidden, weight_down, preferred_element_type=F32).astype(BF16)
    d_hidden = lax.dot_general(rdy, weight_down, LAST, preferred_element_type=F32)
    d_gate = (d_hidden * up_act * sigma * (1.0 + gate_act * (1.0 - sigma))).astype(BF16)
    d_up = (d_hidden * gate_act * sigma).astype(BF16)
    d_rows = lax.dot_general(d_gate, weight_gate, LAST, preferred_element_type=F32)
    d_rows = d_rows + lax.dot_general(d_up, weight_up, LAST, preferred_element_type=F32)
    d_rows = d_rows.astype(BF16)
    made = pl.pallas_call(
        functools.partial(back, n, m, capacity, pad),
        out_shape=(
            shape((chans, tokens), BF16),
            shape((chans, tokens), BF16),
            shape((taps, chans), F32),
            shape((1, chans), F32),
            shape((2, tokens), F32),
            shape(w_gate.shape[1:], BF16),
            shape(w_up.shape[1:], BF16),
            shape(w_down.shape[1:], BF16),
        ),
        in_specs=[vmem] * 18,
        out_specs=(vmem,) * 8,
        scratch_shapes=[
            *[pltpu.VMEM((m, slots, chans), BF16)] * 4,
            pltpu.VMEM((m, tokens, chans), BF16),
            pltpu.VMEM((m, tokens, chans), BF16),
            pltpu.VMEM((m, tokens, chans), BF16),
            pltpu.VMEM((m, tokens, chans), BF16),
            pltpu.VMEM((m, 8, tokens), F32),
            pltpu.VMEM((m, 8, tokens), F32),
            pltpu.VMEM((chans, tokens), BF16),
            pltpu.VMEM((chans, tokens), BF16),
            pltpu.VMEM((chans, tokens), BF16),
            pltpu.VMEM((n, pad, chans), F32),
            *sems((m, n), (m, n), m, m, m, m),
            pltpu.SemaphoreType.DMA((4,)),
            *sems(n),
        ],
        compiler_params=pltpu.CompilerParams(
            collective_id=1, has_side_effects=True, vmem_limit_bytes=40 << 20
        ),
        name="back",
    )(
        result, d_rows, rx, rdy, hidden, d_gate, d_up, inputs, left, right, taps_t, gain_row,
        routes_t, gates_t, grad_out, cots, mixed, scale,
    )
    anywhere = pl.BlockSpec(memory_space=pl.ANY)
    count = len(made)
    layer_out, grad_in, grad_taps, grad_gain, grad_gates, grad_gate, grad_up, grad_down = pl.pallas_call(
        functools.partial(hand_on, count),
        out_shape=tuple(shape(a.shape, a.dtype) for a in made),
        in_specs=[anywhere] * count,
        out_specs=(anywhere,) * count,
        scratch_shapes=[pltpu.SemaphoreType.DMA((count,))],
        name="hand_on",
    )(*made)
    return (
        layer_out,
        grad_in,
        grad_taps.T,
        grad_gain[0],
        grad_gates.T,
        grad_gate[None],
        grad_up[None],
        grad_down[None],
    )


def solution(mesh):
    return jax.shard_map(
        local,
        mesh=mesh,
        in_specs=(
            P("exp", "ctx"),
            P("exp", None),
            P("exp"),
            P("ctx", None),
            P("ctx", None),
            P("ctx", None, "exp"),
            P("ctx", None, "exp"),
            P("ctx", "exp", None),
            P("exp", "ctx"),
        ),
        out_specs=(
            P("exp", "ctx"),
            P("exp", "ctx"),
            P("exp", None),
            P("exp"),
            P("ctx", None),
            P("ctx", None, "exp"),
            P("ctx", None, "exp"),
            P("ctx", "exp", None),
        ),
        check_vma=False,
    )
```
